1024 devices in a mesh: pole: 2 (over z_hi), row: 32 (over x, y, core), col: 16 (over z_lo).
Axes of the slice: x: 4, y: 4, z: 32 (z_hi: 2, z_lo: 16; z = z_hi * 16 + z_lo), core: 2. Of those that a mesh axis runs over, the one named last changes fastest.
Arguments:
- ancestor_inverse: float32 [2, 2, 8192, 8192], P('pole', None, 'col', 'row'), may hold values from -0.0625 to 0.0625
- lower_panel: float32 [2, 2, 8192, 256], P('pole', None, None, 'row'), may hold values from -6 to 6
- pole_weights: float32 [2, 2], P('pole'), may hold values from -1 to 1
- structure: int32 [32, 1], replicated, may hold values 0 or 1
Outputs:
- selected_inverse: float32 [2, 2, 256, 8192], P('pole', None, 'row', 'col')
- density: float32 [256, 8192], P('row')
The draws below stay inside these ranges and needn't reach their ends.
Inputs may be any that keep to these rules, and one draw needn't show every extreme that they name: 1 where an ancestor supernode lies in a level supernode's structure, else 0.
All inputs are finite; a program needn't handle non-finite values.
Results may differ from the reference program's by a relative error of at most 0.000071.
Values sent between devices are 32-bit elements; how exact they have to be, the bound alone decides.
A program may use at most 32 MiB of HBM per device.

```python
import jax
import jax.numpy as jnp
from jax import lax

WIDTH = 256
LEVEL_NODES = 1
POLES = 2
BLOCKS = 32
ANCESTORS = 8192
COLUMNS = 256


def touch_ends(drawn, key, low, top_value):
    shape = drawn.shape
    spot = [jax.random.randint(jax.random.fold_in(key, axis), (), 0, shape[axis]) for axis in range(len(shape))]
    drawn = drawn.at[tuple(spot)].set(low)
    longest = shape.index(max(shape))
    spot[longest] = (spot[longest] + 1) % shape[longest]
    return drawn.at[tuple(spot)].set(top_value)


def levels(key, extent, shards, smallest, largest):
    level, own = 1.0, jax.random.fold_in(key, 6)
    for axis_at, shards_of in shards:
        heights = jnp.exp(jax.random.uniform(jax.random.fold_in(own, axis_at), (shards_of,), jnp.float32, smallest / len(shards), largest / len(shards)))
        level = level * jnp.repeat(heights, extent[axis_at] // shards_of).reshape([-1 if axis == axis_at else 1 for axis in range(len(extent))])
    return level


def scatter_about(stream_key, dims, scale, most, shards=(), held_as=jnp.bfloat16):
    entries = scale * jax.random.normal(stream_key, dims, jnp.float32)
    if shards:
        entries = entries * levels(stream_key, dims, shards, -0.22, 0.18)
    return jnp.clip(entries, -most, most).astype(held_as)


def setup_inputs(seed: int = 0) -> dict:
    arg_keys = jax.random.split(jax.random.key(seed), 5)
    return {
        "ancestor_inverse": scatter_about(arg_keys[0], (POLES, 2, ANCESTORS, ANCESTORS), ANCESTORS ** -0.5, 0.0625, ((0, 2), (2, 16), (3, 32)), jnp.float32),
        "lower_panel": scatter_about(arg_keys[1], (POLES, 2, ANCESTORS, COLUMNS), 1.0, 6.0, ((0, 2), (3, 32)), jnp.float32),
        "pole_weights": jnp.clip(jax.random.uniform(arg_keys[2], (POLES, 2), jnp.float32, -1.0, 1.0) * levels(arg_keys[2], (POLES, 2), ((0, 2),), -0.4, 0.0), -1.0, 1.0),
        "structure": touch_ends((jax.random.randint(arg_keys[3], (BLOCKS, LEVEL_NODES), 0, 4) < 3).astype(jnp.int32), jax.random.fold_in(arg_keys[3], 1), 0, 1),
    }


def expand_structure(structure):
    blocks = structure.astype(jnp.float32)
    return jnp.repeat(jnp.repeat(blocks, WIDTH, axis=0), WIDTH, axis=1)


def reference(ancestor_inverse, lower_panel, pole_weights, structure):
    structure_mask = expand_structure(structure)
    selected = lower_panel * structure_mask[None, None, :, :]

    def pole_inverse(inputs):
        inverse, panel_block = inputs
        real_part = jnp.dot(inverse[0], panel_block[0], precision=lax.Precision.HIGHEST) - jnp.dot(inverse[1], panel_block[1], precision=lax.Precision.HIGHEST)
        imaginary = jnp.dot(inverse[0], panel_block[1], precision=lax.Precision.HIGHEST) + jnp.dot(inverse[1], panel_block[0], precision=lax.Precision.HIGHEST)
        stacked = jnp.stack((-real_part * structure_mask, -imaginary * structure_mask), axis=0)
        return jnp.swapaxes(stacked, 1, 2)

    selected_inverse = lax.map(pole_inverse, (ancestor_inverse, selected))
    density = jnp.sum(pole_weights[:, 0, None, None] * selected_inverse[:, 1] + pole_weights[:, 1, None, None] * selected_inverse[:, 0], axis=0)
    return selected_inverse, density
```

```python
import jax
import jax.numpy as jnp
from jax import lax
from jax.experimental import pallas as pl
from jax.experimental.pallas import tpu as pltpu
from jax.sharding import PartitionSpec as P

MESH = pl.DeviceIdType.MESH
CHIPS = 16
SIDE = 4
DEPTH = 32
COLS = 16
SHARE = 8
K = 256
N = 512
NEAR = (-1, 1, 2)


def split(x):
    high = x.astype(jnp.bfloat16)
    return high, (x - high.astype(jnp.float32)).astype(jnp.bfloat16)


def product(left, right):
    dims = (((1,), (1,)), ((), ()))
    return lax.dot_general(left, right, dims, preferred_element_type=jnp.float32)


def kernel(
    a_hbm, panel_hbm, weights_hbm, structure_hbm, selected_ref, density_ref,
    a_ref, panel_ref, weights_ref, structure_ref, a_high, a_low, s_ref,
    give, keep, got, part, far, pair, chosen,
    load_sem, panel_send, panel_recv, core_send, core_recv, part_send, part_recv,
    far_send, far_recv, near_send, near_recv, store_sem, reach4, reach8,
):
    row = lax.axis_index("row")
    col = lax.axis_index("col")
    z = lax.axis_index("pole") * COLS + col
    chip = lax.div(row, 2)
    core = lax.rem(row, 2)
    x, y = lax.div(chip, SIDE), lax.rem(chip, SIDE)

    def plane(i):
        dx, dy = lax.div(i, SIDE) + 2, lax.rem(i, SIDE) + 2
        return lax.rem(x + dx, SIDE) * SIDE + lax.rem(y + dy, SIDE)

    def along(step):
        other = lax.rem(z + (step % DEPTH), DEPTH)
        return {"pole": lax.div(other, COLS), "col": lax.rem(other, COLS)}

    loads = [
        pltpu.make_async_copy(panel_hbm, panel_ref, load_sem.at[0]),
        pltpu.make_async_copy(a_hbm, a_ref, load_sem.at[1]),
        pltpu.make_async_copy(structure_hbm, structure_ref, load_sem.at[2]),
        pltpu.make_async_copy(weights_hbm, weights_ref, load_sem.at[3]),
    ]
    for load in loads:
        load.start()

    barrier = pltpu.get_barrier_semaphore()
    for step in (-4, 4, -2, 2, -1, 1):
        pl.semaphore_signal(barrier, inc=1, device_id=along(step), device_id_type=MESH)

    own = 2 * CHIPS // 2 + 2 * 2

    def greet(i, _):
        there = plane(lax.div(i, 2)) * 2 + lax.rem(core + lax.rem(i, 2), 2)
        pl.semaphore_signal(barrier, inc=1, device_id={"row": there}, device_id_type=MESH)
        return 0

    lax.fori_loop(0, own, greet, 0)
    lax.fori_loop(own + 1, 2 * CHIPS, greet, 0)
    for load in loads:
        load.wait()
    pl.semaphore_wait(barrier, 2 * CHIPS - 1 + 6)

    def send_panel(i, _):
        there = plane(lax.div(i, 2)) * 2 + lax.rem(core + lax.rem(i, 2), 2)
        pltpu.make_async_remote_copy(
            src_ref=panel_ref.at[:, :, pl.ds(pl.multiple_of(there * K, K), K)],
            dst_ref=s_ref.at[:, core, chip],
            send_sem=panel_send,
            recv_sem=panel_recv,
            device_id={"row": there},
            device_id_type=MESH,
        ).start()
        return 0

    lax.fori_loop(0, own, send_panel, 0)
    lax.fori_loop(own + 1, 2 * CHIPS, send_panel, 0)
    for step in (-4, 4):
        pl.semaphore_signal(reach4, inc=1, device_id=along(step), device_id_type=MESH)

    s_ref[:, core, chip] = panel_ref[:, :, pl.ds(pl.multiple_of(row * K, K), K)]
    row_mask = structure_ref[0, row].astype(jnp.float32)
    high, low = split(a_ref[...] * row_mask)
    a_high[...] = high
    a_low[...] = low

    arrived = panel_ref.at[:, :, pl.ds(0, (2 * CHIPS - 1) * K)]
    pltpu.make_async_copy(arrived, arrived, panel_recv).wait()
    pl.semaphore_wait(reach4, 2)
    for step in (-8, 8):
        pl.semaphore_signal(reach8, inc=1, device_id=along(step), device_id_type=MESH)

    def multiply(which, out):
        parts = []
        for c in range(2):
            parts.append(split(s_ref[c, which].reshape(CHIPS * SHARE, K)))

        def full(s, c):
            return (
                product(s[0], a_high[c]) + product(s[1], a_high[c]) + product(s[0], a_low[c])
            )

        real = full(parts[0], 0) - full(parts[1], 1)
        out[0] = real.reshape(CHIPS, SHARE, N)
        imag = full(parts[1], 0) + full(parts[0], 1)
        out[1] = imag.reshape(CHIPS, SHARE, N)

    multiply(1 - core, give)
    to_core = pltpu.make_async_remote_copy(
        src_ref=give, dst_ref=got, send_sem=core_send, recv_sem=core_recv,
        device_id={"row": chip * 2 + 1 - core}, device_id_type=MESH,
    )
    to_core.start()
    multiply(core, keep)
    to_core.wait_recv()
    keep[...] += got[...]

    mine = CHIPS // 2 + 2

    def send_part(i, _):
        there = plane(i)
        pltpu.make_async_remote_copy(
            src_ref=keep.at[:, there],
            dst_ref=part.at[chip],
            send_sem=part_send,
            recv_sem=part_recv,
            device_id={"row": there * 2 + core},
            device_id_type=MESH,
        ).start()
        return 0

    lax.fori_loop(0, mine, send_part, 0)
    lax.fori_loop(mine + 1, CHIPS, send_part, 0)
    part[chip] = keep[:, chip]
    pltpu.make_async_copy(part.at[pl.ds(1, CHIPS - 1)], part.at[pl.ds(1, CHIPS - 1)], part_recv).wait()

    total = part[0]
    for i in range(1, CHIPS):
        total = total + part[i]
    first = -structure_ref[0, 2 * col].astype(jnp.float32)
    second = -structure_ref[0, 2 * col + 1].astype(jnp.float32)
    chosen[:, :, : N // 2] = total[:, :, : N // 2] * first
    chosen[:, :, N // 2 :] = total[:, :, N // 2 :] * second
    far[0] = weights_ref[0, 0] * chosen[1] + weights_ref[0, 1] * chosen[0]
    pl.semaphore_wait(reach8, 2)
    for m in (4, 3, 5, 2, 6, 1, 7):
        pltpu.make_async_remote_copy(
            src_ref=far.at[0], dst_ref=far.at[8 - m], send_sem=far_send, recv_sem=far_recv,
            device_id=along(4 * m), device_id_type=MESH,
        ).start()
    store = pltpu.make_async_copy(chosen, selected_ref, store_sem.at[0])
    store.start()
    pltpu.make_async_copy(far.at[pl.ds(1, 7)], far.at[pl.ds(1, 7)], far_recv).wait()
    for k in range(4):
        pair[k] = far[k] + far[k + 4]
    for k in range(4):
        place = density_ref.at[:, pl.ds(pl.multiple_of(lax.rem(col + 4 * k, COLS) * N, N), N)]
        for step in NEAR:
            pltpu.make_async_remote_copy(
                src_ref=pair.at[k], dst_ref=place, send_sem=near_send, recv_sem=near_recv,
                device_id=along(step), device_id_type=MESH,
            ).start()
        pltpu.make_async_copy(pair.at[k], place, store_sem.at[1]).start()

    store.wait()
    pltpu.make_async_copy(pair, pair, store_sem.at[1]).wait()
    three = density_ref.at[:, pl.ds(0, 12 * N)]
    pltpu.make_async_copy(three, three, near_recv).wait()
    pltpu.make_async_copy(arrived, arrived, panel_send).wait()
    to_core.wait_send()
    pltpu.make_async_copy(part.at[pl.ds(1, CHIPS - 1)], part.at[pl.ds(1, CHIPS - 1)], part_send).wait()
    pltpu.make_async_copy(far.at[pl.ds(1, 7)], far.at[pl.ds(1, 7)], far_send).wait()
    pltpu.make_async_copy(three, three, near_send).wait()


def local(ancestor_inverse, lower_panel, pole_weights, structure):
    f32, bf16 = jnp.float32, jnp.bfloat16
    dma = pltpu.SemaphoreType.DMA
    selected, density = pl.pallas_call(
        kernel,
        name="level_panel",
        out_shape=(
            jax.ShapeDtypeStruct((2, SHARE, N), f32),
            jax.ShapeDtypeStruct((SHARE, COLS * N), f32),
        ),
        in_specs=[pl.BlockSpec(memory_space=pl.ANY)] * 4,
        out_specs=[pl.BlockSpec(memory_space=pl.ANY)] * 2,
        scratch_shapes=[
            pltpu.VMEM((2, N, K), f32),
            pltpu.VMEM((2, SHARE, 2 * CHIPS * K), f32),
            pltpu.SMEM((1, 2), f32),
            pltpu.SMEM((1, 32), jnp.int32),
            pltpu.VMEM((2, N, K), bf16),
            pltpu.VMEM((2, N, K), bf16),
            pltpu.VMEM((2, 2, CHIPS, SHARE, K), f32),
            pltpu.VMEM((2, CHIPS, SHARE, N), f32),
            pltpu.VMEM((2, CHIPS, SHARE, N), f32),
            pltpu.VMEM((2, CHIPS, SHARE, N), f32),
            pltpu.VMEM((CHIPS, 2, SHARE, N), f32),
            pltpu.VMEM((8, SHARE, N), f32),
            pltpu.VMEM((4, SHARE, N), f32),
            pltpu.VMEM((2, SHARE, N), f32),
            dma((4,)), dma, dma, dma, dma, dma, dma, dma, dma, dma, dma, dma((2,)),
            pltpu.SemaphoreType.REGULAR, pltpu.SemaphoreType.REGULAR,
        ],
        compiler_params=pltpu.CompilerParams(
            collective_id=0, has_side_effects=True, vmem_limit_bytes=60 * 1024 * 1024
        ),
        cost_estimate=pl.CostEstimate(
            flops=3 * 8 * N * K * 256, bytes_accessed=4 << 20, transcendentals=0
        ),
    )(
        ancestor_inverse[0],
        jnp.swapaxes(lower_panel[0], 1, 2),
        pole_weights,
        structure.T,
    )
    return selected[None], density


def solution(mesh):
    return jax.shard_map(
        local,
        mesh=mesh,
        in_specs=(
            P("pole", None, "col", "row"),
            P("pole", None, None, "row"),
            P("pole", None),
            P(),
        ),
        out_specs=(P("pole", None, "row", "col"), P("row", None)),
        check_vma=False,
    )
```

```python
import jax
import jax.numpy as jnp
from jax import lax
from jax.experimental import pallas as pl
from jax.experimental.pallas import tpu as pltpu
from jax.sharding import PartitionSpec as P

MESH = pl.DeviceIdType.MESH
CHIPS = 16
SIDE = 4
DEPTH = 32
COLS = 16
BLOCK = 4
SHIFT = 2
HOLDERS = 8
SHARE = 8
K = 256
N = 512


def split(x):
    high = x.astype(jnp.bfloat16)
    return high, (x - high.astype(jnp.float32)).astype(jnp.bfloat16)


def product(left, right):
    dims = (((1,), (1,)), ((), ()))
    return lax.dot_general(left, right, dims, preferred_element_type=jnp.float32)


def full(left, right):
    return product(left[0], right[0]) + product(left[1], right[0]) + product(left[0], right[1])


def kernel(
    a_hbm, panel_hbm, weights_hbm, structure_hbm, selected_ref, density_ref,
    a_ref, panel_ref, weights_ref, structure_ref, a_high, a_low, b_high, b_low, s_ref,
    give, keep, got, part, give_d, keep_d, got_d, part_d, far, pair,
    load_sem, panel_send, panel_recv, core_send, core_recv, part_send, part_recv,
    core_send_d, core_recv_d, part_send_d, part_recv_d,
    far_send, far_recv, near_send, near_recv, reach4, reach8,
):
    row = lax.axis_index("row")
    pole = lax.axis_index("pole")
    col = lax.axis_index("col")
    z = pole * COLS + col
    chip = lax.div(row, 2)
    core = lax.rem(row, 2)
    x, y = lax.div(chip, SIDE), lax.rem(chip, SIDE)
    shifted = lax.rem(z + SHIFT, DEPTH)
    block, member = lax.div(shifted, BLOCK), lax.rem(shifted, BLOCK)

    def plane(i):
        dx, dy = lax.div(i, SIDE) + 2, lax.rem(i, SIDE) + 2
        return lax.rem(x + dx, SIDE) * SIDE + lax.rem(y + dy, SIDE)

    def ring(other):
        other = lax.rem(other, DEPTH)
        return {"pole": lax.div(other, COLS), "col": lax.rem(other, COLS)}

    loads = [
        pltpu.make_async_copy(panel_hbm, panel_ref, load_sem.at[0]),
        pltpu.make_async_copy(a_hbm, a_ref, load_sem.at[1]),
        pltpu.make_async_copy(structure_hbm, structure_ref, load_sem.at[2]),
        pltpu.make_async_copy(weights_hbm, weights_ref, load_sem.at[3]),
    ]
    for load in loads:
        load.start()

    barrier = pltpu.get_barrier_semaphore()
    own = 2 * CHIPS // 2 + 2 * 2

    def greet(i, _):
        there = plane(lax.div(i, 2)) * 2 + lax.rem(core + lax.rem(i, 2), 2)
        pl.semaphore_signal(barrier, inc=1, device_id={"row": there}, device_id_type=MESH)
        return 0

    lax.fori_loop(0, own, greet, 0)
    lax.fori_loop(own + 1, 2 * CHIPS, greet, 0)
    for step in (1, 2, BLOCK):
        for other in (z + step, z + DEPTH - step):
            pl.semaphore_signal(barrier, inc=1, device_id=ring(other), device_id_type=MESH)
    for load in loads:
        load.wait()
    pl.semaphore_wait(barrier, 2 * CHIPS - 1 + 6)

    def send_panel(i, _):
        there = plane(lax.div(i, 2)) * 2 + lax.rem(core + lax.rem(i, 2), 2)
        pltpu.make_async_remote_copy(
            src_ref=panel_ref.at[:, :, pl.ds(pl.multiple_of(there * K, K), K)],
            dst_ref=s_ref.at[:, core, chip],
            send_sem=panel_send,
            recv_sem=panel_recv,
            device_id={"row": there},
            device_id_type=MESH,
        ).start()
        return 0

    lax.fori_loop(0, own, send_panel, 0)
    lax.fori_loop(own + 1, 2 * CHIPS, send_panel, 0)
    for step in (BLOCK, DEPTH - BLOCK):
        pl.semaphore_signal(reach4, inc=1, device_id=ring(z + step), device_id_type=MESH)

    s_ref[:, core, chip] = panel_ref[:, :, pl.ds(pl.multiple_of(row * K, K), K)]
    row_mask = structure_ref[0, row].astype(jnp.float32)
    w_real, w_imag = weights_ref[0, 0], weights_ref[0, 1]
    a_real, a_imag = a_ref[0] * row_mask, a_ref[1] * row_mask
    b_high[0], b_low[0] = split(w_imag * a_real + w_real * a_imag)
    b_high[1], b_low[1] = split(w_real * a_real - w_imag * a_imag)
    a_high[0], a_low[0] = split(a_real)
    a_high[1], a_low[1] = split(a_imag)
    pl.semaphore_wait(reach4, 2)
    for step in (2 * BLOCK, DEPTH - 2 * BLOCK):
        pl.semaphore_signal(reach8, inc=1, device_id=ring(z + step), device_id_type=MESH)

    arrived = panel_ref.at[:, :, pl.ds(0, (2 * CHIPS - 1) * K)]
    pltpu.make_async_copy(arrived, arrived, panel_recv).wait()

    def pieces(which):
        return [split(s_ref[c, which].reshape(CHIPS * SHARE, K)) for c in range(2)]

    def multiply_d(which, out):
        s = pieces(which)
        value = full(s[0], (b_high[0], b_low[0])) + full(s[1], (b_high[1], b_low[1]))
        out[...] = value.reshape(CHIPS, SHARE, N)

    def multiply(which, out):
        s = pieces(which)
        real, imag = (a_high[0], a_low[0]), (a_high[1], a_low[1])
        out[0] = (full(s[0], real) - full(s[1], imag)).reshape(CHIPS, SHARE, N)
        out[1] = (full(s[1], real) + full(s[0], imag)).reshape(CHIPS, SHARE, N)

    def to_core(source, target, send, recv):
        return pltpu.make_async_remote_copy(
            src_ref=source, dst_ref=target, send_sem=send, recv_sem=recv,
            device_id={"row": chip * 2 + 1 - core}, device_id_type=MESH,
        )

    mine = CHIPS // 2 + 2

    def spread(take, target, send, recv):
        def send_part(i, _):
            there = plane(i)
            pltpu.make_async_remote_copy(
                src_ref=take(there), dst_ref=target.at[chip], send_sem=send, recv_sem=recv,
                device_id={"row": there * 2 + core}, device_id_type=MESH,
            ).start()
            return 0

        lax.fori_loop(0, mine, send_part, 0)
        lax.fori_loop(mine + 1, CHIPS, send_part, 0)

    def rest(ref):
        return ref.at[pl.ds(1, CHIPS - 1)]

    def total(ref):
        value = ref[0]
        for i in range(1, CHIPS):
            value = value + ref[i]
        return value

    multiply_d(1 - core, give_d)
    core_copy_d = to_core(give_d, got_d, core_send_d, core_recv_d)
    core_copy_d.start()
    multiply_d(core, keep_d)
    core_copy_d.wait_recv()
    keep_d[...] += got_d[...]
    spread(lambda there: keep_d.at[there], part_d, part_send_d, part_recv_d)
    part_d[chip] = keep_d[chip]
    multiply(1 - core, give)
    core_copy = to_core(give, got, core_send, core_recv)
    core_copy.start()
    pltpu.make_async_copy(rest(part_d), rest(part_d), part_recv_d).wait()
    first = -structure_ref[0, 2 * col].astype(jnp.float32)
    second = -structure_ref[0, 2 * col + 1].astype(jnp.float32)

    def masked(value):
        half = N // 2
        return jnp.concatenate([value[..., :half] * first, value[..., half:] * second], axis=-1)

    far[block] = masked(total(part_d))

    def send_far(target):
        pltpu.make_async_remote_copy(
            src_ref=far.at[block], dst_ref=far.at[block], send_sem=far_send,
            recv_sem=far_recv.at[block], device_id=ring(target * BLOCK + member + DEPTH - SHIFT),
            device_id_type=MESH,
        ).start()

    def send_far_to(*targets):
        for target in targets:
            pl.when(block != target)(lambda target=target: send_far(target))

    pl.semaphore_wait(reach8, 2)
    send_far_to(0, 1)

    multiply(core, keep)
    send_far_to(2, 3)
    core_copy.wait_recv()
    keep[...] += got[...]
    spread(lambda there: keep.at[:, there], part, part_send, part_recv)
    send_far_to(4, 5, 6, 7)
    part[chip] = keep[:, chip]

    def landed(slot):
        pltpu.make_async_copy(far.at[slot], far.at[slot], far_recv.at[slot]).wait()

    half_ring = HOLDERS // 2
    for step in (2, 1, 3, 0):
        low = lax.rem(block + step, half_ring)
        if step == 0:
            landed(lax.rem(block + half_ring, HOLDERS))
        else:
            landed(low)
            landed(low + half_ring)
        pair[low] = far[low] + far[low + half_ring]
        source = lax.rem(low * BLOCK + member + DEPTH - SHIFT, COLS)
        columns = pl.ds(pl.multiple_of(source * N, N), N)
        place = density_ref.at[:, columns]
        two = 2 + (DEPTH - 4) * (1 - lax.div(lax.rem(low + 1, half_ring), 2))
        for i in (1, DEPTH - 1, two):
            pltpu.make_async_remote_copy(
                src_ref=pair.at[low], dst_ref=place, send_sem=near_send, recv_sem=near_recv,
                device_id=ring(z + i), device_id_type=MESH,
            ).start()
        density_ref[:, columns] = pair[low]

    pltpu.make_async_copy(rest(part), rest(part), part_recv).wait()
    selected_ref[...] = masked(total(part))

    near = density_ref.at[:, pl.ds(0, (COLS - BLOCK) * N)]
    pltpu.make_async_copy(near, near, near_recv).wait()
    pltpu.make_async_copy(arrived, arrived, panel_send).wait()
    core_copy_d.wait_send()
    core_copy.wait_send()
    pltpu.make_async_copy(rest(part_d), rest(part_d), part_send_d).wait()
    pltpu.make_async_copy(rest(part), rest(part), part_send).wait()
    seven = far.at[pl.ds(1, HOLDERS - 1)]
    pltpu.make_async_copy(seven, seven, far_send).wait()
    pltpu.make_async_copy(near, near, near_send).wait()


def finish(selected_in, density_in, selected_out, density_out, sem):
    copies = [
        pltpu.make_async_copy(selected_in, selected_out, sem.at[0]),
        pltpu.make_async_copy(density_in, density_out, sem.at[1]),
    ]
    for copy in copies:
        copy.start()
    for copy in copies:
        copy.wait()


def local(ancestor_inverse, lower_panel, pole_weights, structure):
    f32, bf16 = jnp.float32, jnp.bfloat16
    dma = pltpu.SemaphoreType.DMA
    outputs = ((2, SHARE, N), f32), ((SHARE, COLS * N), f32)
    anywhere = pl.BlockSpec(memory_space=pl.ANY)
    selected, density = pl.pallas_call(
        kernel,
        name="level_panel",
        out_shape=tuple(pltpu.VMEM(*output) for output in outputs),
        in_specs=[anywhere] * 4,
        out_specs=[pl.BlockSpec(memory_space=pltpu.VMEM)] * 2,
        scratch_shapes=[
            pltpu.VMEM((2, N, K), f32),
            pltpu.VMEM((2, SHARE, 2 * CHIPS * K), f32),
            pltpu.SMEM((1, 2), f32),
            pltpu.SMEM((1, 32), jnp.int32),
            pltpu.VMEM((2, N, K), bf16),
            pltpu.VMEM((2, N, K), bf16),
            pltpu.VMEM((2, N, K), bf16),
            pltpu.VMEM((2, N, K), bf16),
            pltpu.VMEM((2, 2, CHIPS, SHARE, K), f32),
            pltpu.VMEM((2, CHIPS, SHARE, N), f32),
            pltpu.VMEM((2, CHIPS, SHARE, N), f32),
            pltpu.VMEM((2, CHIPS, SHARE, N), f32),
            pltpu.VMEM((CHIPS, 2, SHARE, N), f32),
            pltpu.VMEM((CHIPS, SHARE, N), f32),
            pltpu.VMEM((CHIPS, SHARE, N), f32),
            pltpu.VMEM((CHIPS, SHARE, N), f32),
            pltpu.VMEM((CHIPS, SHARE, N), f32),
            pltpu.VMEM((HOLDERS, SHARE, N), f32),
            pltpu.VMEM((HOLDERS // 2, SHARE, N), f32),
            dma((4,)), dma, dma, dma, dma, dma, dma, dma, dma, dma, dma,
            dma, dma((HOLDERS,)), dma, dma,
            pltpu.SemaphoreType.REGULAR, pltpu.SemaphoreType.REGULAR,
        ],
        compiler_params=pltpu.CompilerParams(
            collective_id=0, has_side_effects=True, vmem_limit_bytes=60 * 1024 * 1024
        ),
        cost_estimate=pl.CostEstimate(
            flops=3 * 12 * N * K * 256, bytes_accessed=4 << 20, transcendentals=0
        ),
    )(
        ancestor_inverse[0],
        jnp.swapaxes(lower_panel[0], 1, 2),
        pole_weights,
        structure.T,
    )
    selected, density = pl.pallas_call(
        finish,
        name="store_panels",
        out_shape=tuple(jax.ShapeDtypeStruct(*output) for output in outputs),
        in_specs=[anywhere] * 2,
        out_specs=[anywhere] * 2,
        scratch_shapes=[dma((2,))],
        compiler_params=pltpu.CompilerParams(vmem_limit_bytes=8 * 1024 * 1024),
    )(selected, density)
    return selected[None], density


def solution(mesh):
    return jax.shard_map(
        local,
        mesh=mesh,
        in_specs=(
            P("pole", None, "col", "row"),
            P("pole", None, None, "row"),
            P("pole", None),
            P(),
        ),
        out_specs=(P("pole", None, "row", "col"), P("row", None)),
        check_vma=False,
    )
```

```python
import jax
import jax.numpy as jnp
from jax import lax
from jax.experimental import pallas as pl
from jax.experimental.pallas import tpu as pltpu
from jax.sharding import PartitionSpec as P

MESH = pl.DeviceIdType.MESH
CHIPS = 16
SIDE = 4
HALF = 8
OWN = 10
DEPTH = 32
COLS = 16
BLOCK = 4
SHIFT = 2
HOLDERS = 8
SHARE = 8
K = 256
N = 512


def split(x):
    high = x.astype(jnp.bfloat16)
    return high, (x - high.astype(jnp.float32)).astype(jnp.bfloat16)


def product(left, right):
    dims = (((1,), (0,)), ((), ()))
    return lax.dot_general(left, right, dims, preferred_element_type=jnp.float32)


def full(left, right):
    return product(left[0], right[0]) + product(left[1], right[0]) + product(left[0], right[1])


def kernel(
    a_hbm, panel_hbm, weights_hbm, structure_hbm, selected_ref, density_ref,
    a_ref, panel_ref, weights_ref, structure_ref, a_high, a_low, b_high, b_low, s_ref,
    give, keep, got, part, own_d, got_d, part_d, far, pair,
    load_sem, panel_send, panel_recv, core_send, core_recv, part_send, part_recv,
    core_send_d, core_recv_d, part_send_d, part_recv_d,
    far_send, far_recv, near_send, near_recv, reach4, reach8,
):
    row = lax.axis_index("row")
    pole = lax.axis_index("pole")
    col = lax.axis_index("col")
    z = pole * COLS + col
    chip = lax.div(row, 2)
    core = lax.rem(row, 2)
    x, y = lax.div(chip, SIDE), lax.rem(chip, SIDE)
    shifted = lax.rem(z + SHIFT, DEPTH)
    block, member = lax.div(shifted, BLOCK), lax.rem(shifted, BLOCK)
    agent = core == 1

    def plane(slot):
        dx, dy = lax.div(slot, SIDE) + 2, lax.rem(slot, SIDE) + 2
        return lax.rem(x + dx, SIDE) * SIDE + lax.rem(y + dy, SIDE)

    def back(slot):
        dx, dy = SIDE - lax.div(slot, SIDE), SIDE - lax.rem(slot, SIDE)
        return lax.rem(dx, SIDE) * SIDE + lax.rem(dy, SIDE)

    def ring(other, core_there):
        other = lax.rem(other, DEPTH)
        there = {"pole": lax.div(other, COLS), "col": lax.rem(other, COLS)}
        return {**there, "row": chip * 2 + core_there}

    barrier = pltpu.get_barrier_semaphore()

    def greet(i, _):
        there = plane(lax.div(i, 2)) * 2 + lax.rem(core + lax.rem(i, 2), 2)
        pl.semaphore_signal(barrier, inc=1, device_id={"row": there}, device_id_type=MESH)
        return 0

    def greet_along(*steps):
        for step in steps:
            for other in (z + step, z + DEPTH - step):
                pl.semaphore_signal(
                    barrier, inc=1, device_id=ring(other, 1), device_id_type=MESH
                )

    lax.fori_loop(0, 2 * OWN, greet, 0)
    lax.fori_loop(2 * OWN + 1, 2 * CHIPS, greet, 0)
    greet_along(1, 2)
    pl.when(agent)(lambda: greet_along(BLOCK))
    loads = [
        pltpu.make_async_copy(panel_hbm, panel_ref, load_sem.at[0]),
        pltpu.make_async_copy(a_hbm, a_ref, load_sem.at[1]),
        pltpu.make_async_copy(structure_hbm, structure_ref, load_sem.at[2]),
        pltpu.make_async_copy(weights_hbm, weights_ref, load_sem.at[3]),
    ]
    for load in loads:
        load.start()
    for load in loads:
        load.wait()
    pl.semaphore_wait(barrier, 2 * CHIPS - 1 + 10 * core)

    def send_panel(half):
        def send(i, _):
            slot = lax.div(i, 2)
            there = plane(back(slot)) * 2 + lax.rem(core + lax.rem(i, 2), 2)
            pltpu.make_async_remote_copy(
                src_ref=panel_ref.at[:, :, pl.ds(pl.multiple_of(there * K, K), K)],
                dst_ref=s_ref.at[:, slot, core],
                send_sem=panel_send,
                recv_sem=panel_recv.at[half],
                device_id={"row": there},
                device_id_type=MESH,
            ).start()
            return 0

        return send

    lax.fori_loop(0, CHIPS, send_panel(0), 0)
    lax.fori_loop(CHIPS, 2 * OWN, send_panel(1), 0)
    lax.fori_loop(2 * OWN + 1, 2 * CHIPS, send_panel(1), 0)

    def reach(sem, step):
        for other in (z + step, z + DEPTH - step):
            pl.semaphore_signal(sem, inc=1, device_id=ring(other, 1), device_id_type=MESH)

    pl.when(agent)(lambda: reach(reach4, BLOCK))

    s_ref[:, OWN, core] = panel_ref[:, :, pl.ds(pl.multiple_of(row * K, K), K)]
    row_mask = structure_ref[0, row].astype(jnp.float32)
    w_real, w_imag = weights_ref[0, 0], weights_ref[0, 1]
    a_real, a_imag = a_ref[0].T * row_mask, a_ref[1].T * row_mask
    b_high[0], b_low[0] = split(w_imag * a_real + w_real * a_imag)
    b_high[1], b_low[1] = split(w_real * a_real - w_imag * a_imag)
    a_high[0], a_low[0] = split(a_real)
    a_high[1], a_low[1] = split(a_imag)

    @pl.when(agent)
    def _():
        pl.semaphore_wait(reach4, 2)
        reach(reach8, 2 * BLOCK)

    def arrived(half):
        return panel_ref.at[:, :, pl.ds(0, (CHIPS - half) * K)]

    def multiply_d(half):
        pltpu.make_async_copy(arrived(half), arrived(half), panel_recv.at[half]).wait()
        s = []
        for c in range(2):
            rows = s_ref[c, half * HALF : (half + 1) * HALF]
            s.append(split(rows.reshape(CHIPS * SHARE, K)))
        value = full(s[0], (b_high[0], b_low[0])) + full(s[1], (b_high[1], b_low[1]))
        own_d[half * HALF : (half + 1) * HALF] = value.reshape(HALF, 2, SHARE, N)

    def multiply(which, out):
        s = [split(s_ref[c, :, which].reshape(CHIPS * SHARE, K)) for c in range(2)]
        real, imag = (a_high[0], a_low[0]), (a_high[1], a_low[1])
        out[0] = (full(s[0], real) - full(s[1], imag)).reshape(CHIPS, SHARE, N)
        out[1] = (full(s[1], real) + full(s[0], imag)).reshape(CHIPS, SHARE, N)

    def to_core(source, target, send, recv):
        return pltpu.make_async_remote_copy(
            src_ref=source, dst_ref=target, send_sem=send, recv_sem=recv,
            device_id={"row": chip * 2 + 1 - core}, device_id_type=MESH,
        )

    def spread(first, last, take, target, send, recv):
        def send_part(slot, _):
            pltpu.make_async_remote_copy(
                src_ref=take(slot), dst_ref=target.at[back(slot)], send_sem=send,
                recv_sem=recv, device_id={"row": plane(slot) * 2 + core}, device_id_type=MESH,
            ).start()
            return 0

        lax.fori_loop(first, last, send_part, 0)

    def rest(ref):
        return ref.at[pl.ds(1, CHIPS - 1)]

    def total(ref, first_slot=0):
        value = ref[first_slot]
        for i in range(1, CHIPS):
            value = value + ref[first_slot + i]
        return value

    first = -structure_ref[0, 2 * col].astype(jnp.float32)
    second = -structure_ref[0, 2 * col + 1].astype(jnp.float32)

    def masked(value):
        half = N // 2
        return jnp.concatenate([value[..., :half] * first, value[..., half:] * second], axis=-1)

    def spread_d(first, last):
        def send_part(slot, _):
            pltpu.make_async_remote_copy(
                src_ref=own_d.at[slot, core], dst_ref=part_d.at[core * CHIPS + back(slot)],
                send_sem=part_send_d, recv_sem=part_recv_d,
                device_id={"row": plane(slot) * 2 + 1}, device_id_type=MESH,
            ).start()
            return 0

        lax.fori_loop(first, last, send_part, 0)

    halves = []
    for half in range(2):
        slots = pl.ds(half * HALF, HALF)
        multiply_d(half)
        halves.append(
            to_core(
                own_d.at[slots, 1 - core], got_d.at[slots],
                core_send_d.at[half], core_recv_d.at[half],
            )
        )
        halves[half].start()
    for half in range(2):
        slots = pl.ds(half * HALF, HALF)
        halves[half].wait_recv()
        own_d[slots, core] += got_d[slots]
        if half == 0:
            spread_d(0, HALF)
        else:
            spread_d(HALF, OWN)
            spread_d(OWN + 1, CHIPS)
            pl.when(core == 0)(lambda: spread_d(OWN, OWN + 1))
    d_others = part_d.at[pl.ds(1, 2 * CHIPS - 1)]

    multiply(1 - core, give)
    core_copy = to_core(give, got, core_send, core_recv)
    core_copy.start()

    def send_far(target):
        pltpu.make_async_remote_copy(
            src_ref=far.at[block], dst_ref=far.at[block], send_sem=far_send,
            recv_sem=far_recv.at[block],
            device_id=ring(target * BLOCK + member + DEPTH - SHIFT, 1),
            device_id_type=MESH,
        ).start()

    def send_far_to(*targets):
        for target in targets:
            pl.when(agent & (block != target))(lambda target=target: send_far(target))

    @pl.when(agent)
    def _():
        part_d[CHIPS + OWN] = own_d[OWN, 1]
        pltpu.make_async_copy(d_others, d_others, part_recv_d).wait()
        far[block, 0] = masked(total(part_d, 0))
        far[block, 1] = masked(total(part_d, CHIPS))
        pl.semaphore_wait(reach8, 2)

    send_far_to(0, 1)

    multiply(core, keep)
    send_far_to(2, 3)
    core_copy.wait_recv()
    keep[...] += got[...]
    spread(0, OWN, lambda i: keep.at[:, i], part, part_send, part_recv)
    spread(OWN + 1, CHIPS, lambda i: keep.at[:, i], part, part_send, part_recv)
    send_far_to(4, 5, 6, 7)
    part[OWN] = keep[:, OWN]

    def landed(slot):
        pltpu.make_async_copy(far.at[slot], far.at[slot], far_recv.at[slot]).wait()

    half_ring = HOLDERS // 2

    @pl.when(agent)
    def _():
        for step in (2, 1, 3, 0):
            low = lax.rem(block + step, half_ring)
            if step == 0:
                landed(lax.rem(block + half_ring, HOLDERS))
            else:
                landed(low)
                landed(low + half_ring)
            pair[low] = far[low] + far[low + half_ring]
            source = lax.rem(low * BLOCK + member + DEPTH - SHIFT, COLS)
            columns = pl.ds(pl.multiple_of(source * N, N), N)
            two = 2 + (DEPTH - 4) * (1 - lax.div(lax.rem(low + 1, half_ring), 2))
            for core_there, steps in ((0, (1, DEPTH - 1, two)), (1, (1, DEPTH - 1, two)), (0, (0,))):
                for i in steps:
                    pltpu.make_async_remote_copy(
                        src_ref=pair.at[low, core_there], dst_ref=density_ref.at[:, columns],
                        send_sem=near_send, recv_sem=near_recv,
                        device_id=ring(z + i, core_there), device_id_type=MESH,
                    ).start()
            density_ref[:, columns] = pair[low, 1]

    pltpu.make_async_copy(rest(part), rest(part), part_recv).wait()
    selected_ref[...] = masked(total(part))

    panel_sent = panel_ref.at[:, :, pl.ds(0, (2 * CHIPS - 1) * K)]
    pltpu.make_async_copy(panel_sent, panel_sent, panel_send).wait()
    for half in range(2):
        halves[half].wait_send()
    core_copy.wait_send()
    pltpu.make_async_copy(rest(part), rest(part), part_send).wait()

    @pl.when(core == 0)
    def _():
        pltpu.make_async_copy(got_d, got_d, part_send_d).wait()
        pltpu.make_async_copy(density_ref, density_ref, near_recv).wait()

    @pl.when(agent)
    def _():
        pltpu.make_async_copy(rest(got_d), rest(got_d), part_send_d).wait()
        seven = far.at[pl.ds(1, HOLDERS - 1)]
        pltpu.make_async_copy(seven, seven, far_send).wait()
        near = density_ref.at[:, pl.ds(0, (COLS - BLOCK) * N)]
        pltpu.make_async_copy(near, near, near_recv).wait()
        sent = part_d.at[pl.ds(0, 28)]
        pltpu.make_async_copy(sent, sent, near_send).wait()


def finish(selected_in, density_in, selected_out, density_out, sem):
    copies = [
        pltpu.make_async_copy(selected_in, selected_out, sem.at[0]),
        pltpu.make_async_copy(density_in, density_out, sem.at[1]),
    ]
    for copy in copies:
        copy.start()
    for copy in copies:
        copy.wait()


def local(ancestor_inverse, lower_panel, pole_weights, structure):
    f32, bf16 = jnp.float32, jnp.bfloat16
    dma = pltpu.SemaphoreType.DMA
    outputs = ((2, SHARE, N), f32), ((SHARE, COLS * N), f32)
    anywhere = pl.BlockSpec(memory_space=pl.ANY)
    selected, density = pl.pallas_call(
        kernel,
        name="level_panel",
        out_shape=tuple(pltpu.VMEM(*output) for output in outputs),
        in_specs=[anywhere] * 4,
        out_specs=[pl.BlockSpec(memory_space=pltpu.VMEM)] * 2,
        scratch_shapes=[
            pltpu.VMEM((2, N, K), f32),
            pltpu.VMEM((2, SHARE, 2 * CHIPS * K), f32),
            pltpu.SMEM((1, 2), f32),
            pltpu.SMEM((1, 32), jnp.int32),
            pltpu.VMEM((2, K, N), bf16),
            pltpu.VMEM((2, K, N), bf16),
            pltpu.VMEM((2, K, N), bf16),
            pltpu.VMEM((2, K, N), bf16),
            pltpu.VMEM((2, CHIPS, 2, SHARE, K), f32),
            pltpu.VMEM((2, CHIPS, SHARE, N), f32),
            pltpu.VMEM((2, CHIPS, SHARE, N), f32),
            pltpu.VMEM((2, CHIPS, SHARE, N), f32),
            pltpu.VMEM((CHIPS, 2, SHARE, N), f32),
            pltpu.VMEM((CHIPS, 2, SHARE, N), f32),
            pltpu.VMEM((CHIPS, SHARE, N), f32),
            pltpu.VMEM((2 * CHIPS, SHARE, N), f32),
            pltpu.VMEM((HOLDERS, 2, SHARE, N), f32),
            pltpu.VMEM((HOLDERS // 2, 2, SHARE, N), f32),
            dma((4,)), dma, dma((2,)), dma, dma, dma, dma, dma((2,)), dma((2,)), dma, dma,
            dma, dma((HOLDERS,)), dma, dma,
            pltpu.SemaphoreType.REGULAR, pltpu.SemaphoreType.REGULAR,
        ],
        compiler_params=pltpu.CompilerParams(
            collective_id=0, has_side_effects=True, vmem_limit_bytes=60 * 1024 * 1024
        ),
        cost_estimate=pl.CostEstimate(
            flops=3 * 12 * N * K * 256, bytes_accessed=4 << 20, transcendentals=0
        ),
    )(
        ancestor_inverse[0],
        jnp.swapaxes(lower_panel[0], 1, 2),
        pole_weights,
        structure.T,
    )
    selected, density = pl.pallas_call(
        finish,
        name="store_panels",
        out_shape=tuple(jax.ShapeDtypeStruct(*output) for output in outputs),
        in_specs=[anywhere] * 2,
        out_specs=[anywhere] * 2,
        scratch_shapes=[dma((2,))],
        compiler_params=pltpu.CompilerParams(vmem_limit_bytes=8 * 1024 * 1024),
    )(selected, density)
    return selected[None], density


def solution(mesh):
    return jax.shard_map(
        local,
        mesh=mesh,
        in_specs=(
            P("pole", None, "col", "row"),
            P("pole", None, None, "row"),
            P("pole", None),
            P(),
        ),
        out_specs=(P("pole", None, "row", "col"), P("row", None)),
        check_vma=False,
    )
```

```python
import jax
import jax.numpy as jnp
from jax import lax
from jax.experimental import pallas as pl
from jax.experimental.pallas import tpu as pltpu
from jax.sharding import PartitionSpec as P

MESH = pl.DeviceIdType.MESH
CHIPS = 16
SIDE = 4
HALF = 8
OWN = 10
DEPTH = 32
COLS = 16
BLOCK = 4
SHIFT = 2
HOLDERS = 8
SHARE = 8
K = 256
N = 512


def split(x):
    high = x.astype(jnp.bfloat16)
    return high, (x - high.astype(jnp.float32)).astype(jnp.bfloat16)


def product(left, right):
    dims = (((1,), (0,)), ((), ()))
    return lax.dot_general(left, right, dims, preferred_element_type=jnp.float32)


def full(left, right):
    return product(left[0], right[0]) + product(left[1], right[0]) + product(left[0], right[1])


def kernel(
    a_hbm, panel_hbm, weights_hbm, structure_hbm, selected_ref, density_ref,
    a_ref, panel_ref, weights_ref, structure_ref, a_high, a_low, b_high, b_low, s_ref,
    give, keep, got, part, own_d, got_d, part_d, far, pair,
    load_sem, panel_send, panel_recv, core_send, core_recv, part_send, part_recv,
    core_send_d, core_recv_d, part_send_d, part_recv_d,
    far_send, far_recv, near_send, near_recv, reach4, reach8,
):
    row = lax.axis_index("row")
    pole = lax.axis_index("pole")
    col = lax.axis_index("col")
    z = pole * COLS + col
    chip = lax.div(row, 2)
    core = lax.rem(row, 2)
    x, y = lax.div(chip, SIDE), lax.rem(chip, SIDE)
    shifted = lax.rem(z + SHIFT, DEPTH)
    block, member = lax.div(shifted, BLOCK), lax.rem(shifted, BLOCK)
    agent = core == 1

    def plane(slot):
        dx, dy = slot // SIDE + 2, slot % SIDE + 2
        return lax.rem(x + dx, SIDE) * SIDE + lax.rem(y + dy, SIDE)

    def back(slot):
        return (SIDE - slot // SIDE) % SIDE * SIDE + (SIDE - slot % SIDE) % SIDE

    def ring(other, core_there):
        other = lax.rem(other, DEPTH)
        there = {"pole": lax.div(other, COLS), "col": lax.rem(other, COLS)}
        return {**there, "row": chip * 2 + core_there}

    barrier = pltpu.get_barrier_semaphore()

    def greet(i):
        there = plane(i // 2) * 2 + lax.rem(core + i % 2, 2)
        pl.semaphore_signal(barrier, inc=1, device_id={"row": there}, device_id_type=MESH)

    def greet_along(*steps):
        for step in steps:
            for other in (z + step, z + DEPTH - step):
                pl.semaphore_signal(
                    barrier, inc=1, device_id=ring(other, 1), device_id_type=MESH
                )

    for i in range(2 * CHIPS):
        if i != 2 * OWN:
            greet(i)
    greet_along(1, 2)
    pl.when(agent)(lambda: greet_along(BLOCK))
    loads = [
        pltpu.make_async_copy(panel_hbm, panel_ref, load_sem.at[0]),
        pltpu.make_async_copy(a_hbm, a_ref, load_sem.at[1]),
        pltpu.make_async_copy(structure_hbm, structure_ref, load_sem.at[2]),
        pltpu.make_async_copy(weights_hbm, weights_ref, load_sem.at[3]),
    ]
    for load in loads:
        load.start()
    for load in loads:
        load.wait()
    pl.semaphore_wait(barrier, 2 * CHIPS - 1 + 10 * core)

    def send_panel(i):
        slot = i // 2
        there = plane(back(slot)) * 2 + lax.rem(core + i % 2, 2)
        pltpu.make_async_remote_copy(
            src_ref=panel_ref.at[:, :, pl.ds(pl.multiple_of(there * K, K), K)],
            dst_ref=s_ref.at[:, slot, core],
            send_sem=panel_send,
            recv_sem=panel_recv.at[slot // HALF],
            device_id={"row": there},
            device_id_type=MESH,
        ).start()

    for i in range(2 * CHIPS):
        if i != 2 * OWN:
            send_panel(i)

    def reach(sem, step):
        for other in (z + step, z + DEPTH - step):
            pl.semaphore_signal(sem, inc=1, device_id=ring(other, 1), device_id_type=MESH)

    pl.when(agent)(lambda: reach(reach4, BLOCK))

    s_ref[:, OWN, core] = panel_ref[:, :, pl.ds(pl.multiple_of(row * K, K), K)]
    row_mask = structure_ref[0, row].astype(jnp.float32)
    w_real, w_imag = weights_ref[0, 0], weights_ref[0, 1]
    a_real, a_imag = a_ref[0].T * row_mask, a_ref[1].T * row_mask
    b_high[0], b_low[0] = split(w_imag * a_real + w_real * a_imag)
    b_high[1], b_low[1] = split(w_real * a_real - w_imag * a_imag)
    a_high[0], a_low[0] = split(a_real)
    a_high[1], a_low[1] = split(a_imag)

    @pl.when(agent)
    def _():
        pl.semaphore_wait(reach4, 2)
        reach(reach8, 2 * BLOCK)

    def arrived(half):
        return panel_ref.at[:, :, pl.ds(0, (CHIPS - half) * K)]

    def multiply_d(half):
        pltpu.make_async_copy(arrived(half), arrived(half), panel_recv.at[half]).wait()
        s = []
        for c in range(2):
            rows = s_ref[c, half * HALF : (half + 1) * HALF]
            s.append(split(rows.reshape(CHIPS * SHARE, K)))
        value = full(s[0], (b_high[0], b_low[0])) + full(s[1], (b_high[1], b_low[1]))
        own_d[half * HALF : (half + 1) * HALF] = value.reshape(HALF, 2, SHARE, N)

    def multiply(which, out):
        s = [split(s_ref[c, :, which].reshape(CHIPS * SHARE, K)) for c in range(2)]
        real, imag = (a_high[0], a_low[0]), (a_high[1], a_low[1])
        out[0] = (full(s[0], real) - full(s[1], imag)).reshape(CHIPS, SHARE, N)
        out[1] = (full(s[1], real) + full(s[0], imag)).reshape(CHIPS, SHARE, N)

    def to_core(source, target, send, recv):
        return pltpu.make_async_remote_copy(
            src_ref=source, dst_ref=target, send_sem=send, recv_sem=recv,
            device_id={"row": chip * 2 + 1 - core}, device_id_type=MESH,
        )

    def spread(first, last, take, target, send, recv):
        def send_part(slot, _):
            pltpu.make_async_remote_copy(
                src_ref=take(slot), dst_ref=target.at[back(slot)], send_sem=send,
                recv_sem=recv, device_id={"row": plane(slot) * 2 + core}, device_id_type=MESH,
            ).start()
            return 0

        lax.fori_loop(first, last, send_part, 0)

    def rest(ref):
        return ref.at[pl.ds(1, CHIPS - 1)]

    def total(ref, first_slot=0):
        value = ref[first_slot]
        for i in range(1, CHIPS):
            value = value + ref[first_slot + i]
        return value

    first = -structure_ref[0, 2 * col].astype(jnp.float32)
    second = -structure_ref[0, 2 * col + 1].astype(jnp.float32)

    def masked(value):
        half = N // 2
        return jnp.concatenate([value[..., :half] * first, value[..., half:] * second], axis=-1)

    def spread_d(first, last):
        def send_part(slot, _):
            pltpu.make_async_remote_copy(
                src_ref=own_d.at[slot, core], dst_ref=part_d.at[core * CHIPS + back(slot)],
                send_sem=part_send_d, recv_sem=part_recv_d,
                device_id={"row": plane(slot) * 2 + 1}, device_id_type=MESH,
            ).start()
            return 0

        lax.fori_loop(first, last, send_part, 0)

    halves = []
    for half in range(2):
        slots = pl.ds(half * HALF, HALF)
        multiply_d(half)
        halves.append(
            to_core(
                own_d.at[slots, 1 - core], got_d.at[slots],
                core_send_d.at[half], core_recv_d.at[half],
            )
        )
        halves[half].start()
    for half in range(2):
        slots = pl.ds(half * HALF, HALF)
        halves[half].wait_recv()
        own_d[slots, core] += got_d[slots]
        if half == 0:
            spread_d(0, HALF)
        else:
            spread_d(HALF, OWN)
            spread_d(OWN + 1, CHIPS)
            pl.when(core == 0)(lambda: spread_d(OWN, OWN + 1))
    d_others = part_d.at[pl.ds(1, 2 * CHIPS - 1)]

    multiply(1 - core, give)
    core_copy = to_core(give, got, core_send, core_recv)
    core_copy.start()

    def send_far(target):
        pltpu.make_async_remote_copy(
            src_ref=far.at[block], dst_ref=far.at[block], send_sem=far_send,
            recv_sem=far_recv.at[block],
            device_id=ring(target * BLOCK + member + DEPTH - SHIFT, 1),
            device_id_type=MESH,
        ).start()

    def send_far_to(*targets):
        for target in targets:
            pl.when(agent & (block != target))(lambda target=target: send_far(target))

    @pl.when(agent)
    def _():
        part_d[CHIPS + OWN] = own_d[OWN, 1]
        pltpu.make_async_copy(d_others, d_others, part_recv_d).wait()
        far[block, 0] = masked(total(part_d, 0))
        far[block, 1] = masked(total(part_d, CHIPS))
        pl.semaphore_wait(reach8, 2)

    send_far_to(0, 1)

    multiply(core, keep)
    send_far_to(2, 3)
    core_copy.wait_recv()
    keep[...] += got[...]
    spread(0, OWN, lambda i: keep.at[:, i], part, part_send, part_recv)
    spread(OWN + 1, CHIPS, lambda i: keep.at[:, i], part, part_send, part_recv)
    send_far_to(4, 5, 6, 7)
    part[OWN] = keep[:, OWN]

    def landed(slot):
        pltpu.make_async_copy(far.at[slot], far.at[slot], far_recv.at[slot]).wait()

    half_ring = HOLDERS // 2

    @pl.when(agent)
    def _():
        for step in (2, 1, 3, 0):
            low = lax.rem(block + step, half_ring)
            if step == 0:
                landed(lax.rem(block + half_ring, HOLDERS))
            else:
                landed(low)
                landed(low + half_ring)
            pair[low] = far[low] + far[low + half_ring]
            source = lax.rem(low * BLOCK + member + DEPTH - SHIFT, COLS)
            columns = pl.ds(pl.multiple_of(source * N, N), N)
            two = 2 + (DEPTH - 4) * (1 - lax.div(lax.rem(low + 1, half_ring), 2))
            for core_there, steps in ((0, (1, DEPTH - 1, two)), (1, (1, DEPTH - 1, two)), (0, (0,))):
                for i in steps:
                    pltpu.make_async_remote_copy(
                        src_ref=pair.at[low, core_there], dst_ref=density_ref.at[:, columns],
                        send_sem=near_send, recv_sem=near_recv,
                        device_id=ring(z + i, core_there), device_id_type=MESH,
                    ).start()
            density_ref[:, columns] = pair[low, 1]

    pltpu.make_async_copy(rest(part), rest(part), part_recv).wait()
    selected_ref[...] = masked(total(part))

    panel_sent = panel_ref.at[:, :, pl.ds(0, (2 * CHIPS - 1) * K)]
    pltpu.make_async_copy(panel_sent, panel_sent, panel_send).wait()
    for half in range(2):
        halves[half].wait_send()
    core_copy.wait_send()
    pltpu.make_async_copy(rest(part), rest(part), part_send).wait()

    @pl.when(core == 0)
    def _():
        pltpu.make_async_copy(got_d, got_d, part_send_d).wait()
        pltpu.make_async_copy(density_ref, density_ref, near_recv).wait()

    @pl.when(agent)
    def _():
        pltpu.make_async_copy(rest(got_d), rest(got_d), part_send_d).wait()
        seven = far.at[pl.ds(1, HOLDERS - 1)]
        pltpu.make_async_copy(seven, seven, far_send).wait()
        near = density_ref.at[:, pl.ds(0, (COLS - BLOCK) * N)]
        pltpu.make_async_copy(near, near, near_recv).wait()
        sent = part_d.at[pl.ds(0, 28)]
        pltpu.make_async_copy(sent, sent, near_send).wait()


def finish(selected_in, density_in, selected_out, density_out, sem):
    copies = [
        pltpu.make_async_copy(selected_in, selected_out, sem.at[0]),
        pltpu.make_async_copy(density_in, density_out, sem.at[1]),
    ]
    for copy in copies:
        copy.start()
    for copy in copies:
        copy.wait()


def local(ancestor_inverse, lower_panel, pole_weights, structure):
    f32, bf16 = jnp.float32, jnp.bfloat16
    dma = pltpu.SemaphoreType.DMA
    outputs = ((2, SHARE, N), f32), ((SHARE, COLS * N), f32)
    anywhere = pl.BlockSpec(memory_space=pl.ANY)
    selected, density = pl.pallas_call(
        kernel,
        name="level_panel",
        out_shape=tuple(pltpu.VMEM(*output) for output in outputs),
        in_specs=[anywhere] * 4,
        out_specs=[pl.BlockSpec(memory_space=pltpu.VMEM)] * 2,
        scratch_shapes=[
            pltpu.VMEM((2, N, K), f32),
            pltpu.VMEM((2, SHARE, 2 * CHIPS * K), f32),
            pltpu.SMEM((1, 2), f32),
            pltpu.SMEM((1, 32), jnp.int32),
            pltpu.VMEM((2, K, N), bf16),
            pltpu.VMEM((2, K, N), bf16),
            pltpu.VMEM((2, K, N), bf16),
            pltpu.VMEM((2, K, N), bf16),
            pltpu.VMEM((2, CHIPS, 2, SHARE, K), f32),
            pltpu.VMEM((2, CHIPS, SHARE, N), f32),
            pltpu.VMEM((2, CHIPS, SHARE, N), f32),
            pltpu.VMEM((2, CHIPS, SHARE, N), f32),
            pltpu.VMEM((CHIPS, 2, SHARE, N), f32),
            pltpu.VMEM((CHIPS, 2, SHARE, N), f32),
            pltpu.VMEM((CHIPS, SHARE, N), f32),
            pltpu.VMEM((2 * CHIPS, SHARE, N), f32),
            pltpu.VMEM((HOLDERS, 2, SHARE, N), f32),
            pltpu.VMEM((HOLDERS // 2, 2, SHARE, N), f32),
            dma((4,)), dma, dma((2,)), dma, dma, dma, dma, dma((2,)), dma((2,)), dma, dma,
            dma, dma((HOLDERS,)), dma, dma,
            pltpu.SemaphoreType.REGULAR, pltpu.SemaphoreType.REGULAR,
        ],
        compiler_params=pltpu.CompilerParams(
            collective_id=0, has_side_effects=True, vmem_limit_bytes=60 * 1024 * 1024
        ),
        cost_estimate=pl.CostEstimate(
            flops=3 * 12 * N * K * 256, bytes_accessed=4 << 20, transcendentals=0
        ),
    )(
        ancestor_inverse[0],
        jnp.swapaxes(lower_panel[0], 1, 2),
        pole_weights,
        structure.T,
    )
    selected, density = pl.pallas_call(
        finish,
        name="store_panels",
        out_shape=tuple(jax.ShapeDtypeStruct(*output) for output in outputs),
        in_specs=[anywhere] * 2,
        out_specs=[anywhere] * 2,
        scratch_shapes=[dma((2,))],
        compiler_params=pltpu.CompilerParams(vmem_limit_bytes=8 * 1024 * 1024),
    )(selected, density)
    return selected[None], density


def solution(mesh):
    return jax.shard_map(
        local,
        mesh=mesh,
        in_specs=(
            P("pole", None, "col", "row"),
            P("pole", None, None, "row"),
            P("pole", None),
            P(),
        ),
        out_specs=(P("pole", None, "row", "col"), P("row", None)),
        check_vma=False,
    )
```
